512 devices in a mesh: dp: 32 (over y, x), mp: 16 (over z, core).
Axes of the slice: x: 4, y: 8, z: 8, core: 2. Of those that a mesh axis runs over, the one named last changes fastest.
Arguments:
- activations: bfloat16 [24, 512, 32768], P(None, 'mp', 'dp'), may hold values from -6 to 6
- cotangent: bfloat16 [32768, 1024], P('dp'), may hold values from -0.0078125 to 0.0078125
- slot_blocks: int32 [64], replicated, may hold values from 0 to 48, as said below
- left_stat: float32 [64, 512, 512], P('dp', 'mp'), may hold values from -6 to 48
- right_stat: float32 [64, 512, 512], P('dp', 'mp'), may hold values from -6 to 48
- left_root: bfloat16 [64, 512, 512], P('dp', 'mp'), may hold values from -1 to 1.5
- right_root: bfloat16 [64, 512, 512], P('dp', 'mp'), may hold values from -1 to 1.5
Outputs:
- left_new: float32 [64, 512, 512], P('dp', 'mp')
- right_new: float32 [64, 512, 512], P('dp', 'mp')
- precond: bfloat16 [64, 512, 512], P('dp')
The draws below stay inside these ranges and needn't reach their ends.
Inputs may be any that keep to these rules, and one draw needn't show every extreme that they name: `slot_blocks`: slots k * 2 to k * 2 + 1 belong to owner k. Every block number below 48 stands in exactly one slot; the value 48 marks an empty slot; owners hold different numbers of blocks, and some owner has all 2 slots filled.
All inputs are finite; a program needn't handle non-finite values.
Results may differ from the reference program's by a relative error of at most 0.024.
Values may be sent and summed in bfloat16 or wider, within the bound.
No kernel may reach another device: no remote copies, remote signals or barrier semaphores. Data moves between devices by JAX's collectives and lax.ppermute only.
A program may use at most 192 MiB of HBM per device.

```python
import jax
import jax.numpy as jnp
from jax import lax

BLOCK = 512
COL_BLOCKS = 2
SLOTS = 2
TOK_DEV = 1024
ROW_BLOCKS = 24
TOKENS = 32768
N_DP = 32


def symmetric_draw(key, shape, diag_lo, diag_hi, off_scale):
    key_diag, key_norm = jax.random.split(key, 2)
    gauss = jnp.clip(jax.random.normal(key_norm, shape, jnp.float32), -4.0, 4.0)
    noise = gauss
    mirror = (noise + jnp.swapaxes(noise, 1, 2)) * 0.70710678
    diag_vals = jax.random.uniform(key_diag, shape[:2], jnp.float32, diag_lo, diag_hi)
    row_pos = lax.broadcasted_iota(jnp.int32, shape, 1)
    col_pos = lax.broadcasted_iota(jnp.int32, shape, 2)
    return jnp.where(row_pos == col_pos, diag_vals[:, :, None], off_scale * mirror)


def draw_slot_blocks(key, part):
    key = jax.random.fold_in(key, 11)
    key_owner, key_order, key_blocks = jax.random.split(key, 3)
    slot_total = N_DP * SLOTS
    block_total = ROW_BLOCKS * COL_BLOCKS
    full_owner = jax.random.randint(key_owner, (), 0, N_DP)
    order = jax.random.permutation(key_order, slot_total)
    positions = jnp.arange(slot_total, dtype=jnp.int32)
    scores = jnp.where(positions // SLOTS == full_owner, slot_total + positions, order)
    ranked = jnp.argsort(-scores, stable=True)
    block_order = jax.random.permutation(key_blocks, block_total).astype(jnp.int32)
    filled = jnp.full((slot_total,), block_total, jnp.int32)
    return filled.at[ranked[:block_total]].set(block_order)


def draw_left_stat(key, part):
    key = jax.random.fold_in(key, 21)
    return symmetric_draw(key, (N_DP * SLOTS, BLOCK, BLOCK), 16.0, 48.0, 1.0)


def draw_right_stat(key, part):
    key = jax.random.fold_in(key, 31)
    return symmetric_draw(key, (N_DP * SLOTS, BLOCK, BLOCK), 16.0, 48.0, 1.0)


def draw_left_root(key, part):
    key = jax.random.fold_in(key, 41)
    return symmetric_draw(key, (N_DP * SLOTS, BLOCK, BLOCK), 0.5, 1.5, 0.5 / BLOCK ** 0.5).astype(jnp.bfloat16)


def draw_right_root(key, part):
    key = jax.random.fold_in(key, 51)
    return symmetric_draw(key, (N_DP * SLOTS, BLOCK, BLOCK), 0.5, 1.5, 0.5 / BLOCK ** 0.5).astype(jnp.bfloat16)


def level_of(own_key, dims, cuts, low, top_value):
    factor_of, own = 1.0, jax.random.fold_in(own_key, 6)
    for position, parts in cuts:
        heights = jnp.exp(jax.random.uniform(jax.random.fold_in(own, position), (parts,), jnp.float32, low / len(cuts), top_value / len(cuts)))
        factor_of = factor_of * jnp.repeat(heights, dims[position] // parts).reshape([-1 if axis == position else 1 for axis in range(len(dims))])
    return factor_of


def normal_values(key, dims, width, reach, cuts=(), kind=jnp.bfloat16):
    gain = level_of(key, dims, cuts, -0.22, 0.18) if cuts else 1.0
    values = jax.random.normal(key, dims, jnp.float32) * width * gain
    return jnp.minimum(jnp.maximum(values, -reach), reach).astype(kind)


def setup_inputs(seed: int = 0) -> dict:
    keys = jax.random.split(jax.random.key(seed), 8)
    activations = normal_values(keys[0], (ROW_BLOCKS, BLOCK, TOKENS), 1.0, 6.0, ((1, 16), (2, 32)))
    cotangent = normal_values(keys[1], (TOKENS, COL_BLOCKS * BLOCK), (TOKENS * 16) ** -0.5, 0.0078125, ((0, 32),))
    slot_blocks = draw_slot_blocks(jax.random.fold_in(keys[7], 71), 0)
    left_stat = draw_left_stat(jax.random.fold_in(keys[7], 71), 0)
    right_stat = draw_right_stat(jax.random.fold_in(keys[7], 71), 0)
    left_root = draw_left_root(jax.random.fold_in(keys[7], 71), 0)
    right_root = draw_right_root(jax.random.fold_in(keys[7], 71), 0)
    return {"activations": activations, "cotangent": cotangent, "slot_blocks": slot_blocks, "left_stat": left_stat, "right_stat": right_stat, "left_root": left_root, "right_root": right_root}


decay_factor = 0.95


def reference(activations, cotangent, slot_blocks, left_stat, right_stat, left_root, right_root):
    highest = lax.Precision.HIGHEST
    block_total = ROW_BLOCKS * COL_BLOCKS

    def add_partial(group, running):
        offset = (group * TOK_DEV).astype(jnp.int32)
        act_part = lax.dynamic_slice_in_dim(activations, offset, TOK_DEV, 2).astype(jnp.float32)
        cot_part = lax.dynamic_slice_in_dim(cotangent, offset, TOK_DEV, 0).astype(jnp.float32)
        product = jnp.dot(act_part.reshape(ROW_BLOCKS * BLOCK, TOK_DEV), cot_part, precision=highest)
        rounded = lax.optimization_barrier(product.astype(jnp.bfloat16))
        return running + rounded.astype(jnp.float32)

    summed = lax.fori_loop(0, N_DP, add_partial, jnp.zeros((ROW_BLOCKS * BLOCK, COL_BLOCKS * BLOCK), jnp.float32))
    blocks = summed.reshape(ROW_BLOCKS, BLOCK, COL_BLOCKS, BLOCK).transpose(0, 2, 1, 3).reshape(block_total, BLOCK, BLOCK)
    is_live = slot_blocks < block_total
    clipped = jnp.minimum(slot_blocks, block_total - 1).astype(jnp.int32)
    grad = jnp.where(is_live[:, None, None], jnp.take(blocks, clipped, axis=0), jnp.float32(0.0))
    grad_b = lax.optimization_barrier(grad.astype(jnp.bfloat16)).astype(jnp.float32)
    left_new = decay_factor * left_stat + jnp.einsum("sab,scb->sac", grad_b, grad_b, precision=highest)
    right_new = decay_factor * right_stat + jnp.einsum("sba,sbc->sac", grad_b, grad_b, precision=highest)
    lifted = jnp.einsum("sab,sbc->sac", left_root.astype(jnp.float32), grad_b, precision=highest)
    lifted_b = lax.optimization_barrier(lifted.astype(jnp.bfloat16)).astype(jnp.float32)
    precond = jnp.einsum("sab,sbc->sac", lifted_b, right_root.astype(jnp.float32), precision=highest)
    return left_new, right_new, precond.astype(jnp.bfloat16)
```

```python
import jax
import jax.numpy as jnp
from jax import lax
from jax.experimental import pallas as pl
from jax.experimental.pallas import tpu as pltpu
from jax.sharding import Mesh, PartitionSpec as P

NY, NX, NZ, NC = 8, 4, 8, 2
ROW_BLOCKS, COL_BLOCKS, SLOTS = 24, 2, 2
BLOCKS = ROW_BLOCKS * COL_BLOCKS
ROWS, WIDTH = 32, 512
DECAY = 0.95
STEPS = 4
bf16, f32 = jnp.bfloat16, jnp.float32


def partial_kernel(slots, act, cot, out, blocks):
    step = pl.program_id(0)
    per = ROW_BLOCKS // STEPS
    a = act[...].reshape(per * ROWS, act.shape[2])
    for j in range(COL_BLOCKS):
        part = jnp.dot(a, cot[:, j * WIDTH:(j + 1) * WIDTH], preferred_element_type=f32)
        part = part.astype(bf16).reshape(per, ROWS, WIDTH)
        for i in range(per):
            blocks[(step * per + i) * COL_BLOCKS + j] = part[i]

    @pl.when(step == STEPS - 1)
    def _():
        for x in range(NX):
            for y in range(NY):
                for t in range(SLOTS):
                    b = slots[(y * NX + x) * SLOTS + t]
                    at = (x * NY + y) * SLOTS + t
                    piece = blocks[jnp.minimum(b, BLOCKS - 1)]
                    out[at] = jnp.where(b < BLOCKS, piece, jnp.zeros_like(piece))


def packed_partials(slot_blocks, activations, cotangent):
    tokens = cotangent.shape[0]
    per = ROW_BLOCKS // STEPS
    total = NX * NY * SLOTS
    return pl.pallas_call(
        partial_kernel,
        grid_spec=pltpu.PrefetchScalarGridSpec(
            num_scalar_prefetch=1,
            grid=(STEPS,),
            in_specs=[
                pl.BlockSpec((per, ROWS, tokens), lambda i, s: (i, 0, 0)),
                pl.BlockSpec((tokens, COL_BLOCKS * WIDTH), lambda i, s: (0, 0)),
            ],
            out_specs=pl.BlockSpec((total, ROWS, WIDTH), lambda i, s: (0, 0, 0)),
            scratch_shapes=[pltpu.VMEM((BLOCKS, ROWS, WIDTH), bf16)],
        ),
        out_shape=jax.ShapeDtypeStruct((total, ROWS, WIDTH), bf16),
        compiler_params=pltpu.CompilerParams(vmem_limit_bytes=32 * 2**20),
        cost_estimate=pl.CostEstimate(
            flops=2 * ROW_BLOCKS * ROWS * tokens * COL_BLOCKS * WIDTH, bytes_accessed=6 * 2**20, transcendentals=0
        ),
    )(slot_blocks, activations, cotangent)


def final_kernel(place, g_own, g_other, w_own, w_other, left_stat, right_stat, left_new, right_new, precond, g, w):
    core, me = place[0], place[1]

    def rows(z, c):
        return pl.ds(pl.multiple_of((z * NC + c) * ROWS, ROWS), ROWS)

    for z in range(NZ):
        for s in range(SLOTS):
            g[s, rows(z, core), :] = g_own[z, s]
            g[s, rows(z, 1 - core), :] = g_other[z, s]
            for k in range(2):
                w[k, s, rows(z, core), :] = w_own[z, k, s]
                w[k, s, rows(z, 1 - core), :] = w_other[z, k, s]

    mine = pl.ds(pl.multiple_of(me * ROWS, ROWS), ROWS)
    row_id = lax.broadcasted_iota(jnp.int32, (ROWS, WIDTH), 0) + me * ROWS
    col_id = lax.broadcasted_iota(jnp.int32, (ROWS, WIDTH), 1)
    pick = jnp.where(row_id == col_id, 1.0, 0.0).astype(bf16)
    for s in range(SLOTS):
        grad = g[s]
        both = jnp.concatenate([g[s, mine, :], pick], axis=0)
        wide = lax.dot_general(both, grad, (((1,), (1,)), ((), ())), preferred_element_type=f32)
        left_new[s] = DECAY * left_stat[s] + wide[:ROWS]
        own_cols = wide[ROWS:].astype(bf16)
        right_new[s] = DECAY * right_stat[s] + jnp.dot(own_cols, grad, preferred_element_type=f32)
        lifted = jnp.dot(w[0, s], grad, preferred_element_type=f32).astype(bf16)
        precond[s] = jnp.dot(lifted, w[1, s], preferred_element_type=f32).astype(bf16)


def final(place, g_own, g_other, w_own, w_other, left_stat, right_stat):
    vmem = pl.BlockSpec(memory_space=pltpu.VMEM)
    full = (SLOTS, NZ * NC * ROWS, WIDTH)
    return pl.pallas_call(
        final_kernel,
        in_specs=[pl.BlockSpec(memory_space=pltpu.SMEM)] + [vmem] * 6,
        out_specs=(vmem, vmem, vmem),
        out_shape=(
            jax.ShapeDtypeStruct(left_stat.shape, f32),
            jax.ShapeDtypeStruct(right_stat.shape, f32),
            jax.ShapeDtypeStruct(full, bf16),
        ),
        scratch_shapes=[pltpu.VMEM(full, bf16), pltpu.VMEM((2,) + full, bf16)],
        compiler_params=pltpu.CompilerParams(vmem_limit_bytes=40 * 2**20),
        cost_estimate=pl.CostEstimate(flops=12 * 10**8, bytes_accessed=8 * 2**20, transcendentals=0),
    )(place, g_own, g_other, w_own, w_other, left_stat, right_stat)


def spread(piece):
    own = lax.all_to_all(jnp.broadcast_to(piece[None], (NZ,) + piece.shape), "z", 0, 0, tiled=True)
    return own, lax.ppermute(own, "core", [(0, 1), (1, 0)])


def local(activations, cotangent, slot_blocks, left_stat, right_stat, left_root, right_root):
    w_own, w_other = spread(jnp.stack([left_root, right_root]))
    packed = packed_partials(slot_blocks, activations, cotangent)
    got = lax.all_to_all(packed.reshape(NX, NY * SLOTS, ROWS, WIDTH), "x", 0, 0, tiled=True)
    over_x = jnp.sum(got.astype(f32), axis=0).astype(bf16)
    got = lax.all_to_all(over_x.reshape(NY, SLOTS, ROWS, WIDTH), "y", 0, 0, tiled=True)
    grad_b = jnp.sum(got.astype(f32), axis=0).astype(bf16)
    g_own, g_other = spread(grad_b)
    core = lax.axis_index("core")
    place = jnp.stack([core, lax.axis_index("z") * NC + core]).astype(jnp.int32)
    return final(place, g_own, g_other, w_own, w_other, left_stat, right_stat)


def solution(mesh):
    grid = Mesh(mesh.devices.reshape(NY, NX, NZ, NC), ("y", "x", "z", "core"))
    dp, mp = ("y", "x"), ("z", "core")
    return jax.shard_map(
        local,
        mesh=grid,
        in_specs=(P(None, mp, dp), P(dp, None), P(), P(dp, mp, None), P(dp, mp, None), P(dp, mp, None), P(dp, mp, None)),
        out_specs=(P(dp, mp, None), P(dp, mp, None), P(dp, None, None)),
        check_vma=False,
    )
```

```python
import jax
import jax.numpy as jnp
from jax import lax
from jax.experimental import pallas as pl
from jax.experimental.pallas import tpu as pltpu
from jax.sharding import Mesh, PartitionSpec as P

NYH, NYL, NX, NZ, NC = 4, 2, 4, 8, 2
NEAR = NYL * NX
ROW_BLOCKS, COL_BLOCKS, SLOTS = 24, 2, 2
BLOCKS = ROW_BLOCKS * COL_BLOCKS
ROWS, WIDTH = 32, 512
PARTS = 2
DECAY = 0.95
bf16, f32 = jnp.bfloat16, jnp.float32
MIB = 2**20
VMEM = pl.BlockSpec(memory_space=pltpu.VMEM)
HBM = pl.BlockSpec(memory_space=pltpu.HBM)
SMEM = pl.BlockSpec(memory_space=pltpu.SMEM)


def params(mib):
    return pltpu.CompilerParams(vmem_limit_bytes=mib * MIB)


def cost(flops, size):
    return pl.CostEstimate(flops=flops, bytes_accessed=size, transcendentals=0)


def partial_kernel(slots, act, cot, out, act_v, cot_v, blocks, nothing, act_sem, cot_sem, out_sem):
    tokens = act_v.shape[2]
    per = ROW_BLOCKS // PARTS

    def act_copy(p):
        rows = pl.ds(p * per, per)
        return pltpu.make_async_copy(act.at[rows], act_v.at[rows], act_sem.at[p])

    def cot_copy(j):
        cols = pl.ds(j * WIDTH, WIDTH)
        return pltpu.make_async_copy(cot.at[:, cols], cot_v.at[:, cols], cot_sem.at[j])

    cot_copy(0).start()
    for p in range(PARTS):
        act_copy(p).start()
    for j in range(1, COL_BLOCKS):
        cot_copy(j).start()
    nothing[...] = jnp.zeros_like(nothing)
    for j in range(COL_BLOCKS):
        cot_copy(j).wait()
        for p in range(PARTS):
            if j == 0:
                act_copy(p).wait()
            a = act_v[p * per:(p + 1) * per].reshape(per * ROWS, tokens)
            part = jnp.dot(a, cot_v[:, j * WIDTH:(j + 1) * WIDTH], preferred_element_type=f32)
            part = part.astype(bf16).reshape(per, ROWS, WIDTH)
            for i in range(per):
                blocks[(p * per + i) * COL_BLOCKS + j] = part[i]
        for yh in range(NYH):
            for near in range(NEAR):
                for t in range(SLOTS):
                    b = slots[(yh * NEAR + near) * SLOTS + t]
                    at = (near * NYH + yh) * SLOTS + t

                    @pl.when((b < BLOCKS) & (lax.rem(b, COL_BLOCKS) == j))
                    def _():
                        pltpu.make_async_copy(blocks.at[b], out.at[at], out_sem).start()

                    if j == 0:
                        @pl.when(b >= BLOCKS)
                        def _():
                            pltpu.make_async_copy(nothing, out.at[at], out_sem).start()
    pltpu.make_async_copy(out, out, out_sem).wait()


def packed_partials(slot_blocks, activations, cotangent):
    shape = (NEAR * NYH * SLOTS, ROWS, WIDTH)
    return pl.pallas_call(
        partial_kernel,
        in_specs=[SMEM, HBM, HBM],
        out_specs=HBM,
        out_shape=jax.ShapeDtypeStruct(shape, bf16),
        scratch_shapes=[
            pltpu.VMEM(activations.shape, bf16),
            pltpu.VMEM(cotangent.shape, bf16),
            pltpu.VMEM((BLOCKS, ROWS, WIDTH), bf16),
            pltpu.VMEM((ROWS, WIDTH), bf16),
            pltpu.SemaphoreType.DMA((PARTS,)),
            pltpu.SemaphoreType.DMA((COL_BLOCKS,)),
            pltpu.SemaphoreType.DMA,
        ],
        compiler_params=params(62),
        cost_estimate=cost(2 * activations.size * cotangent.shape[1], 6 * MIB),
    )(slot_blocks, activations, cotangent)


def near_sum_kernel(got, out):
    for at in range(NYH * SLOTS):
        total = got[0, at].astype(f32)
        for n in range(1, NEAR):
            total += got[n, at].astype(f32)
        out[at] = total.astype(bf16)


def near_sum(got):
    return pl.pallas_call(
        near_sum_kernel,
        in_specs=[VMEM],
        out_specs=VMEM,
        out_shape=jax.ShapeDtypeStruct(got.shape[1:], bf16),
        compiler_params=params(16),
        cost_estimate=cost(got.size, 3 * MIB),
    )(got)


def last_sum_kernel(got, out):
    for t in range(SLOTS):
        total = got[0, t].astype(f32)
        for n in range(1, NYH):
            total += got[n, t].astype(f32)
        total = total.astype(bf16)
        for z in range(NZ):
            out[z, t] = total


def last_sum(got):
    return pl.pallas_call(
        last_sum_kernel,
        in_specs=[VMEM],
        out_specs=VMEM,
        out_shape=jax.ShapeDtypeStruct((NZ,) + got.shape[1:], bf16),
        compiler_params=params(8),
        cost_estimate=cost(got.size, MIB),
    )(got)


def rows_of(z, core):
    return pl.ds(pl.multiple_of((z * NC + core) * ROWS, ROWS), ROWS)


def roots_kernel(place, here, far, own, other, w):
    core, z_here = place[0], place[1]
    toward = 1 - 2 * core

    def put(pair, z, first):
        for s in range(SLOTS):
            for k in range(2):
                w[k, s, rows_of(z, first), :] = pair[0, k, s]
                w[k, s, rows_of(z, 1 - first), :] = pair[1, k, s]

    put(here, z_here, core)
    put(far, lax.rem(z_here + NZ // 2, NZ), core)
    for n in range(NZ // 2 - 1):
        by = (n + 1) * toward
        put(own.at[n], lax.rem(z_here - by + NZ, NZ), core)
        put(other.at[n], lax.rem(z_here + by + NZ, NZ), 1 - core)


def whole_roots(place, here, far, own, other):
    return pl.pallas_call(
        roots_kernel,
        in_specs=[SMEM] + [VMEM] * 4,
        out_specs=VMEM,
        out_shape=jax.ShapeDtypeStruct((2, SLOTS, NZ * NC * ROWS, WIDTH), bf16),
        compiler_params=params(16),
        cost_estimate=cost(0, 4 * MIB),
    )(place, here, far, own, other)


def final_kernel(place, g_own, g_other, w, left_stat, right_stat, left_new, right_new, precond, g):
    core, z_here = place[0], place[1]
    for z in range(NZ):
        for s in range(SLOTS):
            g[s, rows_of(z, core), :] = g_own[z, s]
            g[s, rows_of(z, 1 - core), :] = g_other[z, s]
    row_id = lax.broadcasted_iota(jnp.int32, (ROWS, WIDTH), 0) + (z_here * NC + core) * ROWS
    col_id = lax.broadcasted_iota(jnp.int32, (ROWS, WIDTH), 1)
    pick = jnp.where(row_id == col_id, 1.0, 0.0).astype(bf16)
    for s in range(SLOTS):
        grad = g[s]
        both = jnp.concatenate([g[s, rows_of(z_here, core), :], pick], axis=0)
        wide = lax.dot_general(both, grad, (((1,), (1,)), ((), ())), preferred_element_type=f32)
        left_new[s] = DECAY * left_stat[s] + wide[:ROWS]
        own_cols = wide[ROWS:].astype(bf16)
        right_new[s] = DECAY * right_stat[s] + jnp.dot(own_cols, grad, preferred_element_type=f32)
        lifted = jnp.dot(w[0, s], grad, preferred_element_type=f32).astype(bf16)
        precond[s] = jnp.dot(lifted, w[1, s], preferred_element_type=f32).astype(bf16)


def final(place, g_own, g_other, w, left_stat, right_stat):
    full = (SLOTS, NZ * NC * ROWS, WIDTH)
    return pl.pallas_call(
        final_kernel,
        in_specs=[SMEM] + [VMEM] * 5,
        out_specs=(VMEM, VMEM, VMEM),
        out_shape=(
            jax.ShapeDtypeStruct(left_stat.shape, f32),
            jax.ShapeDtypeStruct(right_stat.shape, f32),
            jax.ShapeDtypeStruct(full, bf16),
        ),
        scratch_shapes=[pltpu.VMEM(full, bf16)],
        compiler_params=params(32),
        cost_estimate=cost(12 * 10**8, 8 * MIB),
    )(place, g_own, g_other, w, left_stat, right_stat)


def swap(value):
    return lax.ppermute(value, "core", [(0, 1), (1, 0)])


def jump(value, by):
    pairs = []
    for z in range(NZ):
        for core in range(NC):
            pairs.append((z * NC + core, (z + by * (1 - 2 * core)) % NZ * NC + core))
    return lax.ppermute(value, ("z", "core"), pairs)


def exchange(value, axes):
    return lax.all_to_all(value, axes, 0, 0, tiled=True)


def after(value, *others):
    return lax.optimization_barrier((value,) + others)


def local(activations, cotangent, slot_blocks, left_stat, right_stat, left_root, right_root):
    place = jnp.stack([lax.axis_index("core"), lax.axis_index("z")]).astype(jnp.int32)
    roots = jnp.stack([left_root, right_root])
    pair = jnp.stack([roots, swap(roots)])
    r2 = jump(pair, 2)
    r1 = jump(pair, 1)
    r3 = jump(r2, 1)
    part = packed_partials(slot_blocks, activations, cotangent)
    part = near_sum(exchange(part.reshape(NEAR, NYH * SLOTS, ROWS, WIDTH), ("yl", "x")))
    part, r1, r3 = after(part, r1, r3)
    part = last_sum(exchange(part.reshape(NYH, SLOTS, ROWS, WIDTH), "yh"))
    r4 = jump(r3, 1)
    g_own = exchange(part, "z")
    g_own, r4 = after(g_own, r4)
    own = jnp.stack([r1, r2, r3])
    other = swap(own)
    w = whole_roots(place, pair, r4, own, other)
    return final(place, g_own, swap(g_own), w, left_stat, right_stat)


def solution(mesh):
    grid = Mesh(mesh.devices.reshape(NYH, NYL, NX, NZ, NC), ("yh", "yl", "x", "z", "core"))
    dp, mp = ("yh", "yl", "x"), ("z", "core")
    return jax.shard_map(
        local,
        mesh=grid,
        in_specs=(P(None, mp, dp), P(dp, None), P(), P(dp, mp, None), P(dp, mp, None), P(dp, mp, None), P(dp, mp, None)),
        out_specs=(P(dp, mp, None), P(dp, mp, None), P(dp, None, None)),
        check_vma=False,
    )
```

```python
import jax
import jax.numpy as jnp
from jax import lax
from jax.experimental import pallas as pl
from jax.experimental.pallas import tpu as pltpu
from jax.sharding import Mesh, PartitionSpec as P

NYH, NYL, NX, NZ, NC = 4, 2, 4, 8, 2
NEAR = NYL * NX
ROW_BLOCKS, COL_BLOCKS, SLOTS = 24, 2, 2
BLOCKS = ROW_BLOCKS * COL_BLOCKS
ROWS, WIDTH = 32, 512
HALF, QUARTER = ROWS // NYL, WIDTH // NX
PARTS = 2
DECAY = 0.95
bf16, f32 = jnp.bfloat16, jnp.float32
MIB = 2**20
VMEM = pl.BlockSpec(memory_space=pltpu.VMEM)
HBM = pl.BlockSpec(memory_space=pltpu.HBM)
SMEM = pl.BlockSpec(memory_space=pltpu.SMEM)


def params(mib):
    return pltpu.CompilerParams(vmem_limit_bytes=mib * MIB)


def cost(flops, size):
    return pl.CostEstimate(flops=flops, bytes_accessed=size, transcendentals=0)


def partial_kernel(act, cot, out, act_v, cot_v, cut, act_sem, cot_sem, out_sem):
    tokens = act_v.shape[2]
    per = ROW_BLOCKS // PARTS

    def act_copy(p):
        rows = pl.ds(p * per, per)
        return pltpu.make_async_copy(act.at[rows], act_v.at[rows], act_sem.at[p])

    def cot_copy(j):
        cols = pl.ds(j * WIDTH, WIDTH)
        return pltpu.make_async_copy(cot.at[:, cols], cot_v.at[:, cols], cot_sem.at[j])

    def out_copy(j):
        span = pl.ds(j * ROW_BLOCKS, ROW_BLOCKS)
        return pltpu.make_async_copy(cut.at[:, span], out.at[:, span], out_sem.at[j])

    cot_copy(0).start()
    for p in range(PARTS):
        act_copy(p).start()
    for j in range(1, COL_BLOCKS):
        cot_copy(j).start()
    for j in range(COL_BLOCKS):
        cot_copy(j).wait()
        for p in range(PARTS):
            if j == 0:
                act_copy(p).wait()
            a = act_v[p * per:(p + 1) * per].reshape(per * ROWS, tokens)
            part = jnp.dot(a, cot_v[:, j * WIDTH:(j + 1) * WIDTH], preferred_element_type=f32)
            part = part.astype(bf16).reshape(per, ROWS, WIDTH)
            span = slice(j * ROW_BLOCKS + p * per, j * ROW_BLOCKS + (p + 1) * per)
            for yl in range(NYL):
                for x in range(NX):
                    piece = part[:, yl * HALF:(yl + 1) * HALF, x * QUARTER:(x + 1) * QUARTER]
                    cut[yl * NX + x, span] = piece
        out_copy(j).start()
    for j in range(COL_BLOCKS):
        out_copy(j).wait()


def cut_partials(activations, cotangent):
    shape = (NEAR, BLOCKS, HALF, QUARTER)
    return pl.pallas_call(
        partial_kernel,
        in_specs=[HBM, HBM],
        out_specs=HBM,
        out_shape=jax.ShapeDtypeStruct(shape, bf16),
        scratch_shapes=[
            pltpu.VMEM(activations.shape, bf16),
            pltpu.VMEM(cotangent.shape, bf16),
            pltpu.VMEM(shape, bf16),
            pltpu.SemaphoreType.DMA((PARTS,)),
            pltpu.SemaphoreType.DMA((COL_BLOCKS,)),
            pltpu.SemaphoreType.DMA((COL_BLOCKS,)),
        ],
        compiler_params=params(62),
        cost_estimate=cost(2 * activations.size * cotangent.shape[1], 6 * MIB),
    )(activations, cotangent)


def near_sum_kernel(blocks, got, out, total_v):
    total = got[0].astype(f32)
    for n in range(1, NEAR):
        total += got[n].astype(f32)
    total_v[:BLOCKS] = total.astype(bf16)
    total_v[BLOCKS] = jnp.zeros((HALF, QUARTER), bf16)
    for owner in range(NYH * NEAR):
        for t in range(SLOTS):
            out[owner, t] = total_v[blocks[owner * SLOTS + t]]


def near_sum(blocks, got):
    return pl.pallas_call(
        near_sum_kernel,
        in_specs=[SMEM, VMEM],
        out_specs=VMEM,
        out_shape=jax.ShapeDtypeStruct((NYH * NEAR, SLOTS, HALF, QUARTER), bf16),
        scratch_shapes=[pltpu.VMEM((BLOCKS + 1, HALF, QUARTER), bf16)],
        compiler_params=params(16),
        cost_estimate=cost(got.size, 3 * MIB),
    )(blocks, got)


def last_sum_kernel(got, out, total_v, sem):
    for yl in range(NYL):
        for x in range(NX):
            total = got[yl * NX + x].astype(f32)
            for yh in range(1, NYH):
                total += got[yh * NEAR + yl * NX + x].astype(f32)
            total_v[:, yl * HALF:(yl + 1) * HALF, x * QUARTER:(x + 1) * QUARTER] = total.astype(bf16)
    for z in range(NZ):
        pltpu.make_async_copy(total_v, out.at[z], sem).start()
    pltpu.make_async_copy(out, out, sem).wait()


def last_sum(got):
    shape = (SLOTS, ROWS, WIDTH)
    return pl.pallas_call(
        last_sum_kernel,
        in_specs=[VMEM],
        out_specs=HBM,
        out_shape=jax.ShapeDtypeStruct((NZ,) + shape, bf16),
        scratch_shapes=[pltpu.VMEM(shape, bf16), pltpu.SemaphoreType.DMA],
        compiler_params=params(8),
        cost_estimate=cost(got.size, MIB),
    )(got)


def rows_of(z, core):
    return pl.ds(pl.multiple_of((z * NC + core) * ROWS, ROWS), ROWS)


def roots_kernel(place, here, far, own, other, w):
    core, z_here = place[0], place[1]
    toward = 1 - 2 * core

    def put(pair, z, first):
        for s in range(SLOTS):
            for k in range(2):
                w[k, s, rows_of(z, first), :] = pair[0, k, s]
                w[k, s, rows_of(z, 1 - first), :] = pair[1, k, s]

    put(here, z_here, core)
    put(far, lax.rem(z_here + NZ // 2, NZ), core)
    for n in range(NZ // 2 - 1):
        by = (n + 1) * toward
        put(own.at[n], lax.rem(z_here - by + NZ, NZ), core)
        put(other.at[n], lax.rem(z_here + by + NZ, NZ), 1 - core)


def whole_roots(place, here, far, own, other):
    return pl.pallas_call(
        roots_kernel,
        in_specs=[SMEM] + [VMEM] * 4,
        out_specs=VMEM,
        out_shape=jax.ShapeDtypeStruct((2, SLOTS, NZ * NC * ROWS, WIDTH), bf16),
        compiler_params=params(16),
        cost_estimate=cost(0, 4 * MIB),
    )(place, here, far, own, other)


def final_kernel(place, g_own, g_other, w, left_stat, right_stat, left_new, right_new, precond, g):
    core, z_here = place[0], place[1]
    for z in range(NZ):
        for s in range(SLOTS):
            g[s, rows_of(z, core), :] = g_own[z, s]
            g[s, rows_of(z, 1 - core), :] = g_other[z, s]
    row_id = lax.broadcasted_iota(jnp.int32, (ROWS, WIDTH), 0) + (z_here * NC + core) * ROWS
    col_id = lax.broadcasted_iota(jnp.int32, (ROWS, WIDTH), 1)
    pick = jnp.where(row_id == col_id, 1.0, 0.0).astype(bf16)
    for s in range(SLOTS):
        grad = g[s]
        both = jnp.concatenate([g[s, rows_of(z_here, core), :], pick], axis=0)
        wide = lax.dot_general(both, grad, (((1,), (1,)), ((), ())), preferred_element_type=f32)
        left_new[s] = DECAY * left_stat[s] + wide[:ROWS]
        own_cols = wide[ROWS:].astype(bf16)
        right_new[s] = DECAY * right_stat[s] + jnp.dot(own_cols, grad, preferred_element_type=f32)
        lifted = jnp.dot(w[0, s], grad, preferred_element_type=f32).astype(bf16)
        precond[s] = jnp.dot(lifted, w[1, s], preferred_element_type=f32).astype(bf16)


def final(place, g_own, g_other, w, left_stat, right_stat):
    full = (SLOTS, NZ * NC * ROWS, WIDTH)
    return pl.pallas_call(
        final_kernel,
        in_specs=[SMEM] + [VMEM] * 5,
        out_specs=(VMEM, VMEM, VMEM),
        out_shape=(
            jax.ShapeDtypeStruct(left_stat.shape, f32),
            jax.ShapeDtypeStruct(right_stat.shape, f32),
            jax.ShapeDtypeStruct(full, bf16),
        ),
        scratch_shapes=[pltpu.VMEM(full, bf16)],
        compiler_params=params(32),
        cost_estimate=cost(12 * 10**8, 8 * MIB),
    )(place, g_own, g_other, w, left_stat, right_stat)


def swap(value):
    return lax.ppermute(value, "core", [(0, 1), (1, 0)])


def jump(value, by):
    pairs = []
    for z in range(NZ):
        for core in range(NC):
            pairs.append((z * NC + core, (z + by * (1 - 2 * core)) % NZ * NC + core))
    return lax.ppermute(value, ("z", "core"), pairs)


def exchange(value, axes):
    return lax.all_to_all(value, axes, 0, 0, tiled=True)


def after(value, *others):
    return lax.optimization_barrier((value,) + others)


def local(activations, cotangent, slot_blocks, left_stat, right_stat, left_root, right_root):
    place = jnp.stack([lax.axis_index("core"), lax.axis_index("z")]).astype(jnp.int32)
    roots = jnp.stack([left_root, right_root])
    pair = jnp.stack([roots, swap(roots)])
    r2 = jump(pair, 2)
    r1 = jump(pair, 1)
    part = exchange(cut_partials(activations, cotangent), ("yl", "x"))
    place_of = slot_blocks % COL_BLOCKS * ROW_BLOCKS + slot_blocks // COL_BLOCKS
    part = near_sum(jnp.where(slot_blocks < BLOCKS, place_of, BLOCKS), part)
    part, r2, r1 = after(part, r2, r1)
    r3 = jump(r2, 1)
    part = last_sum(exchange(part, ("yh", "yl", "x")))
    part, r3 = after(part, r3)
    r4 = jump(r3, 1)
    g_own = exchange(part, "z")
    g_own, r4 = after(g_own, r4)
    own = jnp.stack([r1, r2, r3])
    w = whole_roots(place, pair, r4, own, swap(own))
    return final(place, g_own, swap(g_own), w, left_stat, right_stat)


def solution(mesh):
    grid = Mesh(mesh.devices.reshape(NYH, NYL, NX, NZ, NC), ("yh", "yl", "x", "z", "core"))
    dp, mp = ("yh", "yl", "x"), ("z", "core")
    return jax.shard_map(
        local,
        mesh=grid,
        in_specs=(P(None, mp, dp), P(dp, None), P(), P(dp, mp, None), P(dp, mp, None), P(dp, mp, None), P(dp, mp, None)),
        out_specs=(P(dp, mp, None), P(dp, mp, None), P(dp, None, None)),
        check_vma=False,
    )
```

```python
import jax
import jax.numpy as jnp
from jax import lax
from jax.experimental import pallas as pl
from jax.experimental.pallas import tpu as pltpu
from jax.sharding import Mesh, PartitionSpec as P

NY, NX, NZ, NC = 8, 4, 8, 2
PAIR = 2
NEAR = PAIR * PAIR
ROW_BLOCKS, COL_BLOCKS, SLOTS = 24, 2, 2
BLOCKS = ROW_BLOCKS * COL_BLOCKS
ROWS, WIDTH = 32, 512
HALF, SIDE = ROWS // PAIR, WIDTH // PAIR
PARTS = 2
DECAY = 0.95
bf16, f32 = jnp.bfloat16, jnp.float32
MIB = 2**20
VMEM = pl.BlockSpec(memory_space=pltpu.VMEM)
HBM = pl.BlockSpec(memory_space=pltpu.HBM)
SMEM = pl.BlockSpec(memory_space=pltpu.SMEM)


def params(mib):
    return pltpu.CompilerParams(vmem_limit_bytes=mib * MIB)


def cost(flops, size):
    return pl.CostEstimate(flops=flops, bytes_accessed=size, transcendentals=0)


def partial_kernel(act, cot, out, act_v, cot_v, cut, act_sem, cot_sem, out_sem):
    tokens = act_v.shape[2]
    per = ROW_BLOCKS // PARTS

    def act_copy(p):
        rows = pl.ds(p * per, per)
        return pltpu.make_async_copy(act.at[rows], act_v.at[rows], act_sem.at[p])

    def cot_copy(j):
        cols = pl.ds(j * WIDTH, WIDTH)
        return pltpu.make_async_copy(cot.at[:, cols], cot_v.at[:, cols], cot_sem.at[j])

    def out_copy(j):
        span = pl.ds(j * ROW_BLOCKS, ROW_BLOCKS)
        return pltpu.make_async_copy(cut.at[:, span], out.at[:, span], out_sem.at[j])

    cot_copy(0).start()
    for p in range(PARTS):
        act_copy(p).start()
    for j in range(1, COL_BLOCKS):
        cot_copy(j).start()
    for j in range(COL_BLOCKS):
        cot_copy(j).wait()
        for p in range(PARTS):
            if j == 0:
                act_copy(p).wait()
            a = act_v[p * per:(p + 1) * per].reshape(per * ROWS, tokens)
            part = jnp.dot(a, cot_v[:, j * WIDTH:(j + 1) * WIDTH], preferred_element_type=f32)
            part = part.astype(bf16).reshape(per, ROWS, WIDTH)
            span = slice(j * ROW_BLOCKS + p * per, j * ROW_BLOCKS + (p + 1) * per)
            for top in range(PAIR):
                for left in range(PAIR):
                    piece = part[:, top * HALF:(top + 1) * HALF, left * SIDE:(left + 1) * SIDE]
                    cut[top * PAIR + left, span] = piece
        out_copy(j).start()
    for j in range(COL_BLOCKS):
        out_copy(j).wait()


def cut_partials(activations, cotangent):
    shape = (NEAR, BLOCKS, HALF, SIDE)
    return pl.pallas_call(
        partial_kernel,
        in_specs=[HBM, HBM],
        out_specs=HBM,
        out_shape=jax.ShapeDtypeStruct(shape, bf16),
        scratch_shapes=[
            pltpu.VMEM(activations.shape, bf16),
            pltpu.VMEM(cotangent.shape, bf16),
            pltpu.VMEM(shape, bf16),
            pltpu.SemaphoreType.DMA((PARTS,)),
            pltpu.SemaphoreType.DMA((COL_BLOCKS,)),
            pltpu.SemaphoreType.DMA((COL_BLOCKS,)),
        ],
        compiler_params=params(62),
        cost_estimate=cost(2 * activations.size * cotangent.shape[1], 6 * MIB),
    )(activations, cotangent)


def near_sum_kernel(blocks, got, out, total_v):
    total = got[0].astype(f32)
    for n in range(1, NEAR):
        total += got[n].astype(f32)
    total_v[:BLOCKS] = total.astype(bf16)
    total_v[BLOCKS] = jnp.zeros((HALF, SIDE), bf16)
    for owner in range(NY * NX):
        for t in range(SLOTS):
            out[owner, t] = total_v[blocks[owner * SLOTS + t]]


def near_sum(blocks, got):
    return pl.pallas_call(
        near_sum_kernel,
        in_specs=[SMEM, VMEM],
        out_specs=VMEM,
        out_shape=jax.ShapeDtypeStruct((NY * NX, SLOTS, HALF, SIDE), bf16),
        scratch_shapes=[pltpu.VMEM((BLOCKS + 1, HALF, SIDE), bf16)],
        compiler_params=params(16),
        cost_estimate=cost(got.size, 3 * MIB),
    )(blocks, got)


def last_sum_kernel(place, got, out, total_v, sem):
    core = place[0]
    for odd_y in range(PAIR):
        for odd_x in range(PAIR):
            total = jnp.zeros(got.shape[1:], f32)
            for y in range(odd_y, NY, PAIR):
                for x in range(odd_x, NX, PAIR):
                    total += got[y * NX + x].astype(f32)
            row = pl.ds(pl.multiple_of(lax.rem(odd_y + core, PAIR) * HALF, HALF), HALF)
            col = pl.ds(pl.multiple_of(lax.rem(odd_x + core, PAIR) * SIDE, SIDE), SIDE)
            total_v[:, row, col] = total.astype(bf16)
    for z in range(NZ):
        pltpu.make_async_copy(total_v, out.at[z], sem).start()
    pltpu.make_async_copy(out, out, sem).wait()


def last_sum(place, got):
    shape = (SLOTS, ROWS, WIDTH)
    return pl.pallas_call(
        last_sum_kernel,
        in_specs=[SMEM, VMEM],
        out_specs=HBM,
        out_shape=jax.ShapeDtypeStruct((NZ,) + shape, bf16),
        scratch_shapes=[pltpu.VMEM(shape, bf16), pltpu.SemaphoreType.DMA],
        compiler_params=params(8),
        cost_estimate=cost(got.size, MIB),
    )(place, got)


def rows_of(z, core):
    return pl.ds(pl.multiple_of((z * NC + core) * ROWS, ROWS), ROWS)


def roots_kernel(place, here, far, own, other, w):
    core, z_here = place[0], place[1]
    toward = 1 - 2 * core

    def put(pair, z, first):
        for s in range(SLOTS):
            for k in range(2):
                w[k, s, rows_of(z, first), :] = pair[0, k, s]
                w[k, s, rows_of(z, 1 - first), :] = pair[1, k, s]

    put(here, z_here, core)
    put(far, lax.rem(z_here + NZ // 2, NZ), core)
    for n in range(NZ // 2 - 1):
        by = (n + 1) * toward
        put(own.at[n], lax.rem(z_here - by + NZ, NZ), core)
        put(other.at[n], lax.rem(z_here + by + NZ, NZ), 1 - core)


def whole_roots(place, here, far, own, other):
    return pl.pallas_call(
        roots_kernel,
        in_specs=[SMEM] + [VMEM] * 4,
        out_specs=VMEM,
        out_shape=jax.ShapeDtypeStruct((2, SLOTS, NZ * NC * ROWS, WIDTH), bf16),
        compiler_params=params(16),
        cost_estimate=cost(0, 4 * MIB),
    )(place, here, far, own, other)


def final_kernel(place, g_own, g_other, w, left_stat, right_stat, left_new, right_new, precond, g):
    core, z_here = place[0], place[1]
    for z in range(NZ):
        for s in range(SLOTS):
            g[s, rows_of(z, core), :] = g_own[z, s]
            g[s, rows_of(z, 1 - core), :] = g_other[z, s]
    row_id = lax.broadcasted_iota(jnp.int32, (ROWS, WIDTH), 0) + (z_here * NC + core) * ROWS
    col_id = lax.broadcasted_iota(jnp.int32, (ROWS, WIDTH), 1)
    pick = jnp.where(row_id == col_id, 1.0, 0.0).astype(bf16)
    for s in range(SLOTS):
        grad = g[s]
        both = jnp.concatenate([g[s, rows_of(z_here, core), :], pick], axis=0)
        wide = lax.dot_general(both, grad, (((1,), (1,)), ((), ())), preferred_element_type=f32)
        left_new[s] = DECAY * left_stat[s] + wide[:ROWS]
        own_cols = wide[ROWS:].astype(bf16)
        right_new[s] = DECAY * right_stat[s] + jnp.dot(own_cols, grad, preferred_element_type=f32)
        lifted = jnp.dot(w[0, s], grad, preferred_element_type=f32).astype(bf16)
        precond[s] = jnp.dot(lifted, w[1, s], preferred_element_type=f32).astype(bf16)


def final(place, g_own, g_other, w, left_stat, right_stat):
    full = (SLOTS, NZ * NC * ROWS, WIDTH)
    return pl.pallas_call(
        final_kernel,
        in_specs=[SMEM] + [VMEM] * 5,
        out_specs=(VMEM, VMEM, VMEM),
        out_shape=(
            jax.ShapeDtypeStruct(left_stat.shape, f32),
            jax.ShapeDtypeStruct(right_stat.shape, f32),
            jax.ShapeDtypeStruct(full, bf16),
        ),
        scratch_shapes=[pltpu.VMEM(full, bf16)],
        compiler_params=params(32),
        cost_estimate=cost(12 * 10**8, 8 * MIB),
    )(place, g_own, g_other, w, left_stat, right_stat)


def swap(value):
    return lax.ppermute(value, "core", [(0, 1), (1, 0)])


def jump(value, by):
    pairs = []
    for z in range(NZ):
        for core in range(NC):
            pairs.append((z * NC + core, (z + by * (1 - 2 * core)) % NZ * NC + core))
    return lax.ppermute(value, ("z", "core"), pairs)


def exchange(value, axes, groups=None):
    return lax.all_to_all(value, axes, 0, 0, axis_index_groups=groups, tiled=True)


def squares():
    groups = []
    for core in range(NC):
        for y in range(0, NY, PAIR):
            for x in range(0, NX, PAIR):
                members = [((y + core + a) % NY, (x + core + b) % NX) for a in range(PAIR) for b in range(PAIR)]
                groups.append([(my * NX + mx) * NC + core for my, mx in members])
    return groups


def after(value, *others):
    return lax.optimization_barrier((value,) + others)


def local(activations, cotangent, slot_blocks, left_stat, right_stat, left_root, right_root):
    place = jnp.stack([lax.axis_index("core"), lax.axis_index("z")]).astype(jnp.int32)
    roots = jnp.stack([left_root, right_root])
    pair = jnp.stack([roots, swap(roots)])
    r1 = jump(pair, 1)
    part = exchange(cut_partials(activations, cotangent), ("y", "x", "core"), squares())
    place_of = slot_blocks % COL_BLOCKS * ROW_BLOCKS + slot_blocks // COL_BLOCKS
    part = near_sum(jnp.where(slot_blocks < BLOCKS, place_of, BLOCKS), part)
    part, r1 = after(part, r1)
    r2 = jump(r1, 1)
    r3 = jump(r2, 1)
    part = last_sum(place, exchange(part, ("y", "x")))
    part, r2, r3 = after(part, r2, r3)
    r4 = jump(r3, 1)
    g_own = exchange(part, "z")
    g_own, r4 = after(g_own, r4)
    own = jnp.stack([r1, r2, r3])
    w = whole_roots(place, pair, r4, own, swap(own))
    return final(place, g_own, swap(g_own), w, left_stat, right_stat)


def solution(mesh):
    grid = Mesh(mesh.devices.reshape(NY, NX, NZ, NC), ("y", "x", "z", "core"))
    dp, mp = ("y", "x"), ("z", "core")
    return jax.shard_map(
        local,
        mesh=grid,
        in_specs=(P(None, mp, dp), P(dp, None), P(), P(dp, mp, None), P(dp, mp, None), P(dp, mp, None), P(dp, mp, None)),
        out_specs=(P(dp, mp, None), P(dp, mp, None), P(dp, None, None)),
        check_vma=False,
    )
```

```python
import jax
import jax.numpy as jnp
from jax import lax
from jax.experimental import pallas as pl
from jax.experimental.pallas import tpu as pltpu
from jax.sharding import Mesh, PartitionSpec as P

NY, NX, NZ, NC = 8, 4, 8, 2
PAIR = 2
NEAR = PAIR * PAIR
ROW_BLOCKS, COL_BLOCKS, SLOTS = 24, 2, 2
BLOCKS = ROW_BLOCKS * COL_BLOCKS
ROWS, WIDTH = 32, 512
HALF, SIDE = ROWS // PAIR, WIDTH // PAIR
PARTS = 2
DECAY = 0.95
bf16, f32 = jnp.bfloat16, jnp.float32
MIB = 2**20
VMEM = pl.BlockSpec(memory_space=pltpu.VMEM)
HBM = pl.BlockSpec(memory_space=pltpu.HBM)
SMEM = pl.BlockSpec(memory_space=pltpu.SMEM)


def params(mib):
    return pltpu.CompilerParams(vmem_limit_bytes=mib * MIB)


def cost(flops, size):
    return pl.CostEstimate(flops=flops, bytes_accessed=size, transcendentals=0)


def partial_kernel(act, cot, out, act_v, cot_v, cut, act_sem, cot_sem, out_sem):
    tokens = act_v.shape[2]
    per = ROW_BLOCKS // PARTS

    def act_copy(p):
        rows = pl.ds(p * per, per)
        return pltpu.make_async_copy(act.at[rows], act_v.at[rows], act_sem.at[p])

    def cot_copy(j):
        cols = pl.ds(j * WIDTH, WIDTH)
        return pltpu.make_async_copy(cot.at[:, cols], cot_v.at[:, cols], cot_sem.at[j])

    def out_copy(j):
        span = pl.ds(j * ROW_BLOCKS, ROW_BLOCKS)
        return pltpu.make_async_copy(cut.at[:, span], out.at[:, span], out_sem.at[j])

    cot_copy(0).start()
    for p in range(PARTS):
        act_copy(p).start()
    for j in range(1, COL_BLOCKS):
        cot_copy(j).start()
    for j in range(COL_BLOCKS):
        cot_copy(j).wait()
        for p in range(PARTS):
            if j == 0:
                act_copy(p).wait()
            a = act_v[p * per:(p + 1) * per].reshape(per * ROWS, tokens)
            part = jnp.dot(a, cot_v[:, j * WIDTH:(j + 1) * WIDTH], preferred_element_type=f32)
            part = part.astype(bf16).reshape(per, ROWS, WIDTH)
            span = slice(j * ROW_BLOCKS + p * per, j * ROW_BLOCKS + (p + 1) * per)
            for top in range(PAIR):
                for left in range(PAIR):
                    piece = part[:, top * HALF:(top + 1) * HALF, left * SIDE:(left + 1) * SIDE]
                    cut[top * PAIR + left, span] = piece
        out_copy(j).start()
    for j in range(COL_BLOCKS):
        out_copy(j).wait()


def cut_partials(activations, cotangent):
    shape = (NEAR, BLOCKS, HALF, SIDE)
    return pl.pallas_call(
        partial_kernel,
        in_specs=[HBM, HBM],
        out_specs=HBM,
        out_shape=jax.ShapeDtypeStruct(shape, bf16),
        scratch_shapes=[
            pltpu.VMEM(activations.shape, bf16),
            pltpu.VMEM(cotangent.shape, bf16),
            pltpu.VMEM(shape, bf16),
            pltpu.SemaphoreType.DMA((PARTS,)),
            pltpu.SemaphoreType.DMA((COL_BLOCKS,)),
            pltpu.SemaphoreType.DMA((COL_BLOCKS,)),
        ],
        compiler_params=params(62),
        cost_estimate=cost(2 * activations.size * cotangent.shape[1], 6 * MIB),
    )(activations, cotangent)


def near_sum_kernel(blocks, got, out, total_v, slots_v, sem):
    total = got[0].astype(f32)
    for n in range(1, NEAR):
        total += got[n].astype(f32)
    total_v[:BLOCKS] = total.astype(bf16)
    total_v[BLOCKS] = jnp.zeros((HALF, SIDE), bf16)
    for y in range(NY):
        span = pl.ds(y * NX, NX)
        for owner in range(y * NX, (y + 1) * NX):
            for t in range(SLOTS):
                slots_v[owner, t] = total_v[blocks[owner * SLOTS + t]]
        pltpu.make_async_copy(slots_v.at[span], out.at[span], sem).start()
    pltpu.make_async_copy(slots_v, out, sem).wait()


def near_sum(blocks, got):
    shape = (NY * NX, SLOTS, HALF, SIDE)
    return pl.pallas_call(
        near_sum_kernel,
        in_specs=[SMEM, VMEM],
        out_specs=HBM,
        out_shape=jax.ShapeDtypeStruct(shape, bf16),
        scratch_shapes=[
            pltpu.VMEM((BLOCKS + 1, HALF, SIDE), bf16),
            pltpu.VMEM(shape, bf16),
            pltpu.SemaphoreType.DMA,
        ],
        compiler_params=params(16),
        cost_estimate=cost(got.size, 3 * MIB),
    )(blocks, got)


def last_sum_kernel(place, got, out, total_v, sem):
    core = place[0]
    for odd_y in range(PAIR):
        for odd_x in range(PAIR):
            total = jnp.zeros(got.shape[1:], f32)
            for y in range(odd_y, NY, PAIR):
                for x in range(odd_x, NX, PAIR):
                    total += got[y * NX + x].astype(f32)
            total = total.astype(bf16)
            for c in range(NC):
                top, left = (odd_y + c) % PAIR, (odd_x + c) % PAIR

                @pl.when(core == c)
                def _():
                    total_v[:, top * HALF:(top + 1) * HALF, left * SIDE:(left + 1) * SIDE] = total

    for z in range(NZ):
        pltpu.make_async_copy(total_v, out.at[z], sem).start()
    pltpu.make_async_copy(out, out, sem).wait()


def last_sum(place, got):
    shape = (SLOTS, ROWS, WIDTH)
    return pl.pallas_call(
        last_sum_kernel,
        in_specs=[SMEM, VMEM],
        out_specs=HBM,
        out_shape=jax.ShapeDtypeStruct((NZ,) + shape, bf16),
        scratch_shapes=[pltpu.VMEM(shape, bf16), pltpu.SemaphoreType.DMA],
        compiler_params=params(8),
        cost_estimate=cost(got.size, MIB),
    )(place, got)


def rows_of(z, core):
    return pl.ds(pl.multiple_of((z * NC + core) * ROWS, ROWS), ROWS)


def roots_kernel(place, here, far, own, other, w):
    core, z_here = place[0], place[1]
    toward = 1 - 2 * core

    def put(pair, z, first):
        for s in range(SLOTS):
            for k in range(2):
                w[k, s, rows_of(z, first), :] = pair[0, k, s]
                w[k, s, rows_of(z, 1 - first), :] = pair[1, k, s]

    put(here, z_here, core)
    put(far, lax.rem(z_here + NZ // 2, NZ), core)
    for n in range(NZ // 2 - 1):
        by = (n + 1) * toward
        put(own.at[n], lax.rem(z_here - by + NZ, NZ), core)
        put(other.at[n], lax.rem(z_here + by + NZ, NZ), 1 - core)


def whole_roots(place, here, far, own, other):
    return pl.pallas_call(
        roots_kernel,
        in_specs=[SMEM] + [VMEM] * 4,
        out_specs=VMEM,
        out_shape=jax.ShapeDtypeStruct((2, SLOTS, NZ * NC * ROWS, WIDTH), bf16),
        compiler_params=params(16),
        cost_estimate=cost(0, 4 * MIB),
    )(place, here, far, own, other)


def final_kernel(place, g_own, g_other, w, left_stat, right_stat, left_new, right_new, precond, g):
    core, z_here = place[0], place[1]
    for z in range(NZ):
        for s in range(SLOTS):
            g[s, rows_of(z, core), :] = g_own[z, s]
            g[s, rows_of(z, 1 - core), :] = g_other[z, s]
    row_id = lax.broadcasted_iota(jnp.int32, (ROWS, WIDTH), 0) + (z_here * NC + core) * ROWS
    col_id = lax.broadcasted_iota(jnp.int32, (ROWS, WIDTH), 1)
    pick = jnp.where(row_id == col_id, 1.0, 0.0).astype(bf16)
    for s in range(SLOTS):
        grad = g[s]
        both = jnp.concatenate([g[s, rows_of(z_here, core), :], pick], axis=0)
        wide = lax.dot_general(both, grad, (((1,), (1,)), ((), ())), preferred_element_type=f32)
        left_new[s] = DECAY * left_stat[s] + wide[:ROWS]
        own_cols = wide[ROWS:].astype(bf16)
        right_new[s] = DECAY * right_stat[s] + jnp.dot(own_cols, grad, preferred_element_type=f32)
        lifted = jnp.dot(w[0, s], grad, preferred_element_type=f32).astype(bf16)
        precond[s] = jnp.dot(lifted, w[1, s], preferred_element_type=f32).astype(bf16)


def final(place, g_own, g_other, w, left_stat, right_stat):
    full = (SLOTS, NZ * NC * ROWS, WIDTH)
    return pl.pallas_call(
        final_kernel,
        in_specs=[SMEM] + [VMEM] * 5,
        out_specs=(VMEM, VMEM, VMEM),
        out_shape=(
            jax.ShapeDtypeStruct(left_stat.shape, f32),
            jax.ShapeDtypeStruct(right_stat.shape, f32),
            jax.ShapeDtypeStruct(full, bf16),
        ),
        scratch_shapes=[pltpu.VMEM(full, bf16)],
        compiler_params=params(32),
        cost_estimate=cost(12 * 10**8, 8 * MIB),
    )(place, g_own, g_other, w, left_stat, right_stat)


def swap(value):
    return lax.ppermute(value, "core", [(0, 1), (1, 0)])


def jump(value, by):
    pairs = []
    for z in range(NZ):
        for core in range(NC):
            pairs.append((z * NC + core, (z + by * (1 - 2 * core)) % NZ * NC + core))
    return lax.ppermute(value, ("z", "core"), pairs)


def exchange(value, axes, groups=None):
    return lax.all_to_all(value, axes, 0, 0, axis_index_groups=groups, tiled=True)


def squares():
    groups = []
    for core in range(NC):
        for y in range(0, NY, PAIR):
            for x in range(0, NX, PAIR):
                members = [((y + core + a) % NY, (x + core + b) % NX) for a in range(PAIR) for b in range(PAIR)]
                groups.append([(my * NX + mx) * NC + core for my, mx in members])
    return groups


def after(value, *others):
    return lax.optimization_barrier((value,) + others)


def local(activations, cotangent, slot_blocks, left_stat, right_stat, left_root, right_root):
    place = jnp.stack([lax.axis_index("core"), lax.axis_index("z")]).astype(jnp.int32)
    roots = jnp.stack([left_root, right_root])
    pair = jnp.stack([roots, swap(roots)])
    r1 = jump(pair, 1)
    part = exchange(cut_partials(activations, cotangent), ("y", "x", "core"), squares())
    place_of = slot_blocks % COL_BLOCKS * ROW_BLOCKS + slot_blocks // COL_BLOCKS
    part = near_sum(jnp.where(slot_blocks < BLOCKS, place_of, BLOCKS), part)
    part, r1 = after(part, r1)
    r2 = jump(r1, 1)
    r3 = jump(r1, 2)
    part = last_sum(place, exchange(part, ("y", "x")))
    part, r2, r3 = after(part, r2, r3)
    r4 = jump(r3, 1)
    g_own = exchange(part, "z")
    g_own, r4 = after(g_own, r4)
    own = jnp.stack([r1, r2, r3])
    w = whole_roots(place, pair, r4, own, swap(own))
    return final(place, g_own, swap(g_own), w, left_stat, right_stat)


def solution(mesh):
    grid = Mesh(mesh.devices.reshape(NY, NX, NZ, NC), ("y", "x", "z", "core"))
    dp, mp = ("y", "x"), ("z", "core")
    return jax.shard_map(
        local,
        mesh=grid,
        in_specs=(P(None, mp, dp), P(dp, None), P(), P(dp, mp, None), P(dp, mp, None), P(dp, mp, None), P(dp, mp, None)),
        out_specs=(P(dp, mp, None), P(dp, mp, None), P(dp, None, None)),
        check_vma=False,
    )
```
